32 devices in a mesh: dp: 8 (over z, x), mp: 4 (over y, core).
Axes of the slice: x: 2, y: 2, z: 4, core: 2. Of those that a mesh axis runs over, the one named last changes fastest.
Arguments:
- tokens: bfloat16 [12288, 768], P('dp'), may hold values from -6 to 6
- cotangent: bfloat16 [12288, 768], P('dp'), may hold values from -6 to 6
- lengths: int32 [24], P('dp'), may hold values from 1 to 512, as said below
- attn_weights: float32 [4, 768, 768], P(None, 'dp', 'mp')
- ffn_weights: float32 [2, 768, 3072], P(None, 'dp', 'mp')
- row_vectors: float32 [6, 768], replicated
- head_bias: float32 [2, 768], P(None, 'mp'), may hold values from -1.5 to 1.5
- up_bias: float32 [3072], P('mp'), may hold values from -1.5 to 1.5
- attn_row_state: float32 [4, 768], P(None, 'dp'), may hold values from 614.4 to 4915.2
- attn_col_state: float32 [4, 768], P(None, 'mp'), may hold values from 614.4 to 4915.2
- ffn_row_state: float32 [2, 768], P(None, 'dp'), may hold values from 614.4 to 4915.2
- ffn_col_state: float32 [2, 3072], P(None, 'mp'), may hold values from 614.4 to 4915.2
- vec_state: float32 [6, 768], replicated, may hold values from 614.4 to 4915.2
- head_bias_state: float32 [2, 768], P(None, 'mp'), may hold values from 614.4 to 4915.2
- up_bias_state: float32 [3072], P('mp'), may hold values from 614.4 to 4915.2
Outputs:
- out: bfloat16 [12288, 768], P('dp')
- grad_input: float32 [12288, 768], P('dp')
- attn_grad: float32 [4, 768, 768], P(None, 'dp', 'mp')
- attn_new: float32 [4, 768, 768], P(None, 'dp', 'mp')
- attn_row_new: float32 [4, 768], P(None, 'dp')
- attn_col_new: float32 [4, 768], P(None, 'mp')
- ffn_grad: float32 [2, 768, 3072], P(None, 'dp', 'mp')
- ffn_new: float32 [2, 768, 3072], P(None, 'dp', 'mp')
- ffn_row_new: float32 [2, 768], P(None, 'dp')
- ffn_col_new: float32 [2, 3072], P(None, 'mp')
- vec_grad: float32 [6, 768], replicated
- vec_state_new: float32 [6, 768], replicated
- vec_new: float32 [6, 768], replicated
- head_bias_grad: float32 [2, 768], P(None, 'mp')
- head_bias_state_new: float32 [2, 768], P(None, 'mp')
- head_bias_new: float32 [2, 768], P(None, 'mp')
- up_bias_grad: float32 [3072], P('mp')
- up_bias_state_new: float32 [3072], P('mp')
- up_bias_new: float32 [3072], P('mp')
The draws below stay inside these ranges and needn't reach their ends.
Inputs may be any that keep to these rules, and one draw needn't show every extreme that they name: `lengths`: every draw holds one sequence of 512 valid keys and one of a single key; most are far shorter.
All inputs are finite; a program needn't handle non-finite values.
Results may differ from the reference program's by a relative error of at most 0.014.
Values may be sent and summed in bfloat16 or wider, within the bound.
A program may use at most 128 MiB of HBM per device.

```python
import math
import jax
import jax.numpy as jnp
from jax import lax

D = 768
HEADS = 12
HD = 64
FF = 3072
SEQ = 512
STEP = 5
SEQS = 24
TOKENS = 12288


def draw_lengths(key, part):
    key = jax.random.fold_in(key, 17)
    level_key, value_key, place_key = jax.random.split(key, 3)
    levels = jax.random.randint(level_key, (SEQS,), 0, SEQ.bit_length())
    spans = jnp.left_shift(jnp.ones((SEQS,), jnp.int32), levels)
    raw_draw = jax.random.randint(value_key, (SEQS,), 0, SEQ)
    lengths = raw_draw % spans + 1
    chosen = jax.random.randint(place_key, (), 0, SEQS)
    lengths = lengths.at[chosen].set(SEQ)
    lengths = lengths.at[(chosen + 1) % SEQS].set(1)
    return lengths.astype(jnp.int32)


def rising_factor(count, top_ratio):
    position = jnp.arange(count, dtype=jnp.float32) / (count - 1)
    slope = top_ratio - 1.0
    mean_square = 1.0 + slope + slope * slope / 3.0
    return (1.0 + slope * position) / jnp.sqrt(mean_square)


def draw_attn_weights(key, part):
    key = jax.random.fold_in(key, 11)
    normal_draw = jax.random.truncated_normal(key, -4.0, 4.0, (4, D, D), jnp.float32)
    slice_scale = jnp.where(jnp.arange(4) == 3, (D // 8) ** (-0.5), D ** (-0.5))
    along = rising_factor(D, 3.0)
    return normal_draw * slice_scale[:, None, None] * along[None, :, None]


def draw_ffn_weights(key, part):
    key = jax.random.fold_in(key, 13)
    normal_draw = jax.random.truncated_normal(key, -4.0, 4.0, (2, D, FF), jnp.float32)
    slice_scale = jnp.where(jnp.arange(2) == 1, FF ** (-0.5), D ** (-0.5))
    along = rising_factor(D, 3.0)
    return normal_draw * slice_scale[:, None, None] * along[None, :, None]


def draw_row_vectors(key, part):
    key = jax.random.fold_in(key, 19)
    gain_key, shift_key = jax.random.split(key)
    gains = jax.random.uniform(gain_key, (6, D), jnp.float32, 0.7, 1.3)
    shifts = 0.3 * jax.random.truncated_normal(shift_key, -4.0, 4.0, (6, D), jnp.float32)
    is_gain = (jnp.arange(6) == 1) | (jnp.arange(6) == 4)
    return jnp.where(is_gain[:, None], gains, shifts)


def block_levels(rng, shape, cuts, least, high):
    def one(dim, shards_of):
        steps = jax.random.uniform(jax.random.fold_in(jax.random.fold_in(rng, 6), dim), (shards_of,), jnp.float32, least / len(cuts), high / len(cuts))
        return jnp.repeat(jnp.exp(steps), shape[dim] // shards_of).reshape((-1,) + (1,) * (len(shape) - dim - 1))

    level = one(*cuts[0])
    for cut in cuts[1:]:
        level = level * one(*cut)
    return level


def gaussian(rng, shape, scale, limit, pieces=(), kind=jnp.bfloat16):
    drawn = jax.random.normal(rng, shape, jnp.float32) * scale
    if len(pieces) > 0:
        drawn = block_levels(rng, shape, pieces, -0.22, 0.18) * drawn
    return jnp.clip(drawn, min=-limit, max=limit).astype(kind)


def setup_inputs(seed: int = 0) -> dict:
    splits = jax.random.split(jax.random.key(seed), 16)
    return {
        "tokens": gaussian(splits[0], (TOKENS, D), 1.0, 6.0, ((0, 8),)),
        "cotangent": gaussian(splits[1], (TOKENS, D), 1.0, 6.0, ((0, 8),)),
        "lengths": draw_lengths(jax.random.fold_in(splits[15], 71), 0),
        "attn_weights": draw_attn_weights(jax.random.fold_in(splits[15], 71), 0),
        "ffn_weights": draw_ffn_weights(jax.random.fold_in(splits[15], 71), 0),
        "row_vectors": draw_row_vectors(jax.random.fold_in(splits[15], 71), 0),
        "head_bias": gaussian(splits[6], (2, D), 0.3, 1.5, ((1, 4),), jnp.float32),
        "up_bias": gaussian(splits[7], (FF,), 0.3, 1.5, ((0, 4),), jnp.float32),
        "attn_row_state": jnp.clip(jnp.exp(math.log(4915.2) - 2.0794415 * jax.random.uniform(splits[8], (4, D), jnp.float32) ** block_levels(splits[8], (4, D), ((1, 8),), -0.2, 0.2)), 614.4, 4915.2),
        "attn_col_state": jnp.clip(jnp.exp(math.log(4915.2) - 2.0794415 * jax.random.uniform(splits[9], (4, D), jnp.float32) ** block_levels(splits[9], (4, D), ((1, 4),), -0.2, 0.2)), 614.4, 4915.2),
        "ffn_row_state": jnp.clip(jnp.exp(math.log(4915.2) - 2.0794415 * jax.random.uniform(splits[10], (2, D), jnp.float32) ** block_levels(splits[10], (2, D), ((1, 8),), -0.2, 0.2)), 614.4, 4915.2),
        "ffn_col_state": jnp.clip(jnp.exp(math.log(4915.2) - 2.0794415 * jax.random.uniform(splits[11], (2, FF), jnp.float32) ** block_levels(splits[11], (2, FF), ((1, 4),), -0.2, 0.2)), 614.4, 4915.2),
        "vec_state": jnp.clip(jnp.exp(jax.random.uniform(splits[12], (6, D), jnp.float32, math.log(614.4), math.log(4915.2))), 614.4, 4915.2),
        "head_bias_state": jnp.clip(jnp.exp(math.log(4915.2) - 2.0794415 * jax.random.uniform(splits[13], (2, D), jnp.float32) ** block_levels(splits[13], (2, D), ((1, 4),), -0.2, 0.2)), 614.4, 4915.2),
        "up_bias_state": jnp.clip(jnp.exp(math.log(4915.2) - 2.0794415 * jax.random.uniform(splits[14], (FF,), jnp.float32) ** block_levels(splits[14], (FF,), ((0, 4),), -0.2, 0.2)), 614.4, 4915.2),
    }


rate = 3.0
clip_limit = 0.1

@jax.custom_vjp
def low(v):
    return lax.optimization_barrier(v.astype(jnp.bfloat16)).astype(jnp.float32)

@jax.custom_vjp
def low_back(v):
    return v

def low_keep(v):
    return (low(v), None)

def low_pass(kept, grad):
    return (grad,)

def back_keep(v):
    return (v, None)

def back_low(kept, grad):
    return (low(grad),)
low.defvjp(low_keep, low_pass)
low_back.defvjp(back_keep, back_low)

def matmul(left, right):
    return jnp.dot(left, right, precision=lax.Precision.HIGHEST)

def layer_norm(summed, norm_gain, norm_shift):
    average = lax.optimization_barrier(jnp.mean(summed, axis=-1, keepdims=True))
    centered = summed - average
    variance = lax.optimization_barrier(jnp.mean(centered * centered, axis=-1, keepdims=True))
    return centered * lax.rsqrt(variance + 1e-12) * norm_gain + norm_shift

def gelu_exact(argument):
    return jax.nn.gelu(argument, approximate=False)

def seq_attention(queries, key_rows, values, length):
    score_scale = 1.0 / math.sqrt(HD)
    scores = jnp.einsum('qhd,khd->hqk', queries, key_rows, precision=lax.Precision.HIGHEST) * score_scale
    scores = low_back(scores)
    visible = lax.broadcasted_iota(jnp.int32, (1, 1, SEQ), 2) < length.astype(jnp.int32)
    scores = jnp.where(visible, scores, -1000000000.0)
    attn_probs = jax.nn.softmax(scores, axis=-1)
    return jnp.einsum('hqk,khd->qhd', low(attn_probs), values, precision=lax.Precision.HIGHEST)

def block_forward(weights, row_block, lengths):
    attn_low, ffn_low, vec_params, head_params, up_params = weights
    seq_count = lengths.shape[0]
    split_shape = (seq_count, SEQ, HEADS, HD)
    queries = low(low_back(matmul(row_block, attn_low[0]) + head_params[0]))
    key_rows = low(low_back(matmul(row_block, attn_low[1])))
    values = low(low_back(matmul(row_block, attn_low[2]) + head_params[1]))
    mixed = jax.vmap(seq_attention)(queries.reshape(split_shape), key_rows.reshape(split_shape), values.reshape(split_shape), lengths)
    mixed = low(low_back(mixed.reshape(seq_count * SEQ, D)))
    attended = low_back(matmul(mixed, attn_low[3].T) + vec_params[0])
    normed = layer_norm(row_block + attended, vec_params[1], vec_params[2])
    hidden = low_back(matmul(low(normed), ffn_low[0]) + up_params)
    activated = low(gelu_exact(hidden))
    branch = low_back(matmul(activated, ffn_low[1].T) + vec_params[3])
    return layer_norm(normed + branch, vec_params[4], vec_params[5])

def finish(weight, update):
    clip_factor = jnp.maximum(1.0, jnp.sqrt(jnp.mean(update * update)) / clip_limit)
    step_size = jnp.maximum(0.001, jnp.sqrt(jnp.mean(weight * weight)))
    return weight - rate * step_size * update / clip_factor

def factored(weight, gradient, row_state, col_state):
    decay_rate = 1.0 - STEP ** (-0.8)
    square = gradient * gradient + 1e-30
    row_new = decay_rate * row_state + (1.0 - decay_rate) * lax.optimization_barrier(jnp.mean(square, axis=1))
    col_new = decay_rate * col_state + (1.0 - decay_rate) * lax.optimization_barrier(jnp.mean(square, axis=0))
    estimate = row_new[:, None] * col_new[None, :] / jnp.mean(row_new)
    return (finish(weight, gradient * lax.rsqrt(estimate)), row_new, col_new)

def vector_update(weight, gradient, prior_state):
    decay_rate = 1.0 - STEP ** (-0.8)
    state_new = decay_rate * prior_state + (1.0 - decay_rate) * (gradient * gradient + 1e-30)
    return (finish(weight, gradient * lax.rsqrt(state_new)), state_new)

def reference(tokens, cotangent, lengths, attn_weights, ffn_weights, row_vectors, head_bias, up_bias, attn_row_state, attn_col_state, ffn_row_state, ffn_col_state, vec_state, head_bias_state, up_bias_state):
    rows_all = tokens.astype(jnp.float32)
    group_size = math.gcd(SEQS, 8)
    blocks = SEQS // group_size
    block_step = jax.checkpoint(block_forward)

    def forward(row_input, attn_master, ffn_master, vec_params, head_params, up_params):
        weights = (low(attn_master), low(ffn_master), vec_params, head_params, up_params)

        def apply_block(element):
            return block_step(weights, element[0], element[1])
        result = lax.map(apply_block, (row_input.reshape(blocks, group_size * SEQ, D), lengths.reshape(blocks, group_size)))
        return result.reshape(TOKENS, D)
    result, pullback = jax.vjp(forward, rows_all, attn_weights, ffn_weights, row_vectors, head_bias, up_bias)
    grad_input, attn_grad, ffn_grad, vec_grad, head_grad, up_grad = pullback(cotangent.astype(jnp.float32))
    attn_new, attn_row_new, attn_col_new = jax.vmap(factored)(attn_weights, attn_grad, attn_row_state, attn_col_state)
    ffn_new, ffn_row_new, ffn_col_new = jax.vmap(factored)(ffn_weights, ffn_grad, ffn_row_state, ffn_col_state)
    vec_new, vec_state_new = jax.vmap(vector_update)(row_vectors, vec_grad, vec_state)
    head_new, head_state_new = jax.vmap(vector_update)(head_bias, head_grad, head_bias_state)
    up_new, up_state_new = vector_update(up_bias, up_grad, up_bias_state)
    return (result.astype(jnp.bfloat16), grad_input, attn_grad, attn_new, attn_row_new, attn_col_new, ffn_grad, ffn_new, ffn_row_new, ffn_col_new, vec_grad, vec_state_new, vec_new, head_grad, head_state_new, head_new, up_grad, up_state_new, up_new)
```

```python
import functools
import math

import jax
import jax.numpy as jnp
from jax import lax
from jax.experimental import pallas as pl
from jax.experimental.pallas import tpu as pltpu
from jax.sharding import PartitionSpec as P

D = 768
HD = 64
FF = 3072
SEQ = 512
STEP = 5
HALF = SEQ // 2


rate = 3.0
clip_limit = 0.1

F32 = jnp.float32
BF = jnp.bfloat16
MESH = pl.DeviceIdType.MESH
VMEM_BYTES = 62 * 1024 * 1024


def dot(left, right):
    return jnp.dot(left, right, preferred_element_type=F32)


def dot_last(left, right):
    return lax.dot_general(left, right, (((1,), (1,)), ((), ())), preferred_element_type=F32)


def dot_first(left, right):
    return lax.dot_general(left, right, (((0,), (0,)), ((), ())), preferred_element_type=F32)


class Place:
    def __init__(self):
        self.d = lax.axis_index("dp")
        self.m = lax.axis_index("mp")
        self.z, self.x = lax.div(self.d, 2), lax.rem(self.d, 2)
        self.y, self.c = lax.div(self.m, 2), lax.rem(self.m, 2)
        self.sibling = (self.d, 2 * self.y + 1 - self.c)
        self.across = (self.d, 2 * (1 - self.y) + self.c)
        self.diagonal = (self.d, 2 * (1 - self.y) + 1 - self.c)
        self.beside = (2 * self.z + 1 - self.x, self.m)

    def along(self, k):
        return (2 * lax.rem(self.z + k, 4) + self.x, self.m)

    def behind(self, k):
        return 2 * lax.rem(self.z + 4 - k, 4) + self.x

    def ahead(self, k, x):
        return 2 * lax.rem(self.z + k, 4) + x


def greet(peers):
    barrier = pltpu.get_barrier_semaphore()
    for peer in peers:
        pl.semaphore_signal(barrier, inc=1, device_id=peer, device_id_type=MESH)
    pl.semaphore_wait(barrier, len(peers))


def push(src, dst, send, recv, peer):
    return pltpu.make_async_remote_copy(
        src_ref=src, dst_ref=dst, send_sem=send, recv_sem=recv, device_id=peer, device_id_type=MESH
    )


def rows_of(start, size):
    return pl.ds(pl.multiple_of(start, size), size)


def head_mask(h, dtype):
    lanes = lax.broadcasted_iota(jnp.int32, (1, 3 * HD), 1)
    return ((lanes >= h * HD) & (lanes < (h + 1) * HD)).astype(F32).astype(dtype)


def norm_parts(summed):
    average = jnp.sum(summed, axis=1, keepdims=True) * (1.0 / D)
    centered = summed - average
    variance = jnp.sum(centered * centered, axis=1, keepdims=True) * (1.0 / D)
    scale = lax.rsqrt(variance + 1e-12)
    return centered * scale, scale


def norm_back(grad, gain, normal, scale):
    weighted = grad * gain
    mean_grad = jnp.sum(weighted, axis=1, keepdims=True) * (1.0 / D)
    mean_along = jnp.sum(weighted * normal, axis=1, keepdims=True) * (1.0 / D)
    return (weighted - mean_grad - normal * mean_along) * scale


def col_sum(v):
    return jnp.sum(v, axis=0, keepdims=True)


class Refs:
    def __init__(self, names, refs):
        self.__dict__.update(zip(names, refs))


def fetched(names, r, sems):
    return {
        name: pltpu.make_async_copy(r.__dict__["far_" + name], r.__dict__[name], sems.at[i])
        for i, name in enumerate(names)
    }


VEC_ROWS = 48
COL_ROWS = 24


def adafactor_rates():
    decay = 1.0 - STEP ** (-0.8)
    return decay, 1.0 - decay


def sum_all(v):
    return jnp.sum(jnp.sum(v, axis=1, keepdims=True), axis=0, keepdims=True)


def new_moments(r, cols, rows):
    decay, keep = adafactor_rates()
    arow = decay * r.ars[...] + keep * (rows[0:4, 0:96] * (1.0 / D))
    frow = decay * r.frs[...] + keep * (rows[4:6, 0:96] * (1.0 / FF))
    col_sums = []
    for i in range(4):
        first = cols[12 + 2 * i : 13 + 2 * i]
        second = cols[13 + 2 * i : 14 + 2 * i, 0:64]
        col_sums.append(jnp.concatenate([first, second], axis=1))
    for i in range(2):
        col_sums.append(jnp.concatenate([cols[6 * i + k : 6 * i + k + 1] for k in range(6)], axis=1))
    states = [r.acs[i : i + 1] for i in range(4)] + [r.fcs[i : i + 1] for i in range(2)]
    col_new = [decay * s + keep * (t * (1.0 / D)) for s, t in zip(states, col_sums)]
    return arow, frow, col_new


def bias_steps(r, cols, vecs):
    decay, keep = adafactor_rates()
    head = jnp.concatenate(
        [
            jnp.concatenate([cols[20 + 2 * i : 21 + 2 * i], cols[21 + 2 * i : 22 + 2 * i, 0:64]], axis=1)
            for i in range(2)
        ],
        axis=0,
    )
    up = jnp.concatenate([vecs[36 + k : 37 + k] for k in range(6)], axis=1)
    head_state = decay * r.hst[...] + keep * (head * head + 1e-30)
    up_state = decay * r.ust[...].reshape(1, D) + keep * (up * up + 1e-30)
    return head, head_state, head * lax.rsqrt(head_state), up, up_state, up * lax.rsqrt(up_state)


MAIN_SMALL = ("aw", "fw", "vec", "hb", "ars", "acs", "frs", "fcs", "hst")
MAIN_IN = ("tokens", "cotangent", "lengths", "ub", "ust") + tuple("far_" + name for name in MAIN_SMALL)
MAIN_OUT = (
    "out",
    "gi",
    "asum",
    "fsum",
    "sums",
)


def main_scratch(n_seq):
    rows = n_seq * SEQ
    own_rows = n_seq * HALF
    wide = 3 * HD

    def low_box(*shape):
        return pltpu.VMEM(shape, BF)

    def box(*shape):
        return pltpu.VMEM(shape, F32)

    return dict(
        small=dma(len(MAIN_SMALL)),
        aw=box(4, 96, wide),
        fw=box(2, 96, D),
        vec=box(6, D),
        hb=box(2, wide),
        ars=box(4, 96),
        acs=box(4, wide),
        frs=box(2, 96),
        fcs=box(2, D),
        hst=box(2, wide),
        xv=low_box(rows, D),
        cv=low_box(n_seq, HALF, D),
        wa=low_box(3, D, wide),
        wf=low_box(2, 8, 96, D),
        wo_all=low_box(4, D, 256),
        qkv=low_box(3, rows, wide),
        probs=low_box(6 * n_seq, SEQ, HALF),
        mixed=low_box(rows, 256),
        o_all=low_box(4, n_seq, HALF, 256),
        low=low_box(rows, D),
        normal=box(own_rows, D),
        scale=box(own_rows, 128),
        z=low_box(rows, D),
        gp=box(rows, D),
        own=box(2, HALF, D),
        csend=low_box(n_seq, HALF, D),
        crecv=low_box(n_seq, HALF, D),
        ysend=low_box(n_seq, HALF, D),
        yrecv=low_box(2, n_seq, HALF, D),
        df=low_box(rows, D),
        dr=box(own_rows, D),
        da=low_box(rows, D),
        du=low_box(SEQ, D),
        dwf=box(2, 8, 96, D),
        fxr=low_box(2, 4, 96, D),
        fzr=low_box(2, 3, 96, D),
        axr=low_box(4, 96, D),
        azr=low_box(3, 96, D),
        pair=box(96, D),
        dk=box(SEQ, wide),
        dv=box(SEQ, wide),
        dqkv=low_box(SEQ, D),
        turned=low_box(wide, SEQ),
        pulls=box(2, SEQ, HALF),
        do=low_box(SEQ, wide),
        vecp=box(8, D),
        vbox=box(8, D),
        vec8=box(6, 8, D),
        up8=box(8, D),
        head8=box(8, D),
        vecbox=box(8, VEC_ROWS, 128),
        colbox=box(8, COL_ROWS, 128),
        rowbox=box(4, 8, 128),
        statm=box(4, 8, 128),
        statd=box(8, 8, 128),
        flip=box(128, 128),
        loads=dma(2, n_seq),
        zs=dma(2, 4, 3), zr=dma(2, 4, 3), xs=dma(4, 4), xr=dma(4, 4), ws=dma(3), wr=dma(3),
        osnd=dma(3, n_seq), orcv=dma(3, n_seq), hs=dma(n_seq), hr=dma(n_seq),
        css=dma(3, n_seq), crs=dma(3, n_seq), yss=dma(3, n_seq), yrs=dma(3, n_seq),
        outs=dma(n_seq), outr=dma(n_seq), outl=dma(n_seq),
        dfs=dma(n_seq), dfr=dma(n_seq), das=dma(n_seq), dar=dma(n_seq),
        gs=dma(n_seq), gr=dma(n_seq), gl=dma(n_seq), go=dma(n_seq),
        fxss=dma(2, 4), fxrs=dma(2, 4), fzss=dma(2, 3), fzrs=dma(2, 3),
        axss=dma(4), axrs=dma(4), azss=dma(3), azrs=dma(3),
        vss=dma(), vrs=dma(), vds=dma(7), vdr=dma(7), cds=dma(7), cdr=dma(7),
        rms=dma(3), rmr=dma(3), sms=dma(3), smr=dma(3), sds=dma(7), sdr=dma(7),
    )


def main_kernel(n_seq, names, *refs):
    r = Refs(names, refs)
    at = Place()
    wide = 3 * HD
    mp_peers = (at.sibling, at.across, at.diagonal)

    def dp_peer(k):
        return (lax.rem(at.d + k, 8), at.m)

    def mp_peer(k):
        return (at.d, lax.rem(at.m + k, 4))

    def my_rows(s):
        return rows_of(s * SEQ + at.c * HALF, HALF)

    def half_of(t):
        return 1 - at.c + t * (2 * at.c - 1)

    def mine(s):
        return rows_of(s * HALF, HALF)

    def seq(s):
        return rows_of(s * SEQ, SEQ)

    def x_load(s):
        return pltpu.make_async_copy(r.tokens.at[seq(s)], r.xv.at[seq(s)], r.loads.at[0, s])

    def c_load(s):
        return pltpu.make_async_copy(r.cotangent.at[my_rows(s)], r.cv.at[s], r.loads.at[1, s])

    small = fetched(MAIN_SMALL, r, r.small)
    for one in small.values():
        one.start()
    for s in range(n_seq):
        x_load(s).start()
    for s in range(n_seq):
        c_load(s).start()
    greet([dp_peer(k) for k in range(1, 8)] + list(mp_peers))

    def shard(j):
        return pl.ds(pl.multiple_of(j * 96, 32), 96)

    def slot(g, j):
        if g == 0:
            return r.da.at[shard(j), pl.ds(0, 640)]
        if g == 1:
            return r.da.at[shard(j), pl.ds(640, 128)]
        return r.wf.at[g - 2, j]

    def right_copy(g, h):
        block = slot(g, 2 * (at.z - h) + at.x)
        return push(block, block, r.zs.at[0, g, h], r.zr.at[0, g, h], (at.d + 2, at.m))

    def left_copy(g, h):
        block = slot(g, 2 * (at.z + h) + at.x)
        return push(block, block, r.zs.at[1, g, h], r.zr.at[1, g, h], (at.d - 2, at.m))

    def x_copy(g, z):
        block = slot(g, 2 * z + at.x)
        return push(block, block, r.xs.at[g, z], r.xr.at[g, z], at.beside)

    def begin(g):
        @pl.when(at.z < 3)
        def _():
            right_copy(g, 0).start()

        @pl.when(at.z > 0)
        def _():
            left_copy(g, 0).start()

    def step(g, h):
        @pl.when(at.z > h)
        def _():
            right_copy(g, h).wait_recv()
            x_copy(g, at.z - 1 - h).start()

        if h < 2:

            @pl.when((at.z > h) & (at.z < 3))
            def _():
                right_copy(g, h + 1).start()

        @pl.when(at.z < 3 - h)
        def _():
            left_copy(g, h).wait_recv()
            x_copy(g, at.z + 1 + h).start()

        if h < 2:

            @pl.when((at.z < 3 - h) & (at.z > 0))
            def _():
                left_copy(g, h + 1).start()

    def sent(g):
        for h in range(3):

            @pl.when((at.z >= h) & (at.z < 3))
            def _():
                right_copy(g, h).wait_send()

            @pl.when((at.z <= 3 - h) & (at.z > 0))
            def _():
                left_copy(g, h).wait_send()

        for z in range(4):
            x_copy(g, z).wait_send()

    def arrived(g):
        for z in range(4):
            x_copy(g, z).wait_recv()

    def pad_lanes(v):
        return jnp.concatenate([v, jnp.zeros((v.shape[0], 256 - wide), v.dtype)], axis=1)

    def wo_copy(i):
        if i < 2:
            block = r.wo_all.at[at.m]
            return push(block, block, r.ws.at[i], r.wr.at[i], mp_peers[i])
        block = r.wo_all.at[at.across[1]]
        return push(block, block, r.ws.at[i], r.wr.at[i], at.sibling)

    def spread_wo():
        arrived(1)
        r.wo_all[at.m] = pad_lanes(r.da[0:D, 3 * wide : 4 * wide])
        for i in (1, 0):
            wo_copy(i).start()

    def hand_on_wo():
        wo_copy(1).wait_recv()
        wo_copy(2).start()

    def o_copy(i, s):
        half = (1 - at.c, at.c, 1 - at.c)[i]
        rows = rows_of(s * SEQ + half * HALF, HALF)
        return push(r.mixed.at[rows], r.o_all.at[at.m, s], r.osnd.at[i, s], r.orcv.at[i, s], mp_peers[i])

    def half_copy(ref, send, recv, s):
        return push(ref.at[my_rows(s)], ref.at[my_rows(s)], send.at[s], recv.at[s], at.sibling)

    def low_copy(s):
        return half_copy(r.low, r.hs, r.hr, s)

    def df_copy(s):
        return half_copy(r.df, r.dfs, r.dfr, s)

    def da_copy(s):
        return half_copy(r.da, r.das, r.dar, s)

    def core_copy(e, s):
        return push(r.csend.at[s], r.crecv.at[s], r.css.at[e, s], r.crs.at[e, s], at.sibling)

    def far_copy(e, s):
        return push(
            r.ysend.at[s], r.yrecv.at[e % 2, s], r.yss.at[e, s], r.yrs.at[e, s], at.across
        )

    def send_part(e, s, part):
        if e > 0:
            core_copy(e - 1, s).wait_send()
        r.csend[s] = part.astype(BF)
        core_copy(e, s).start()

    def pass_on(e, s):
        core_copy(e, s).wait_recv()
        if e > 0:
            far_copy(e - 1, s).wait_send()
        r.ysend[s] = (r.own[s % 2] + r.crecv[s].astype(F32)).astype(BF)
        far_copy(e, s).start()

    def whole(e, s):
        far_copy(e, s).wait_recv()
        return r.ysend[s].astype(F32) + r.yrecv[e % 2, s].astype(F32)

    def project_in(s):
        x_rows = r.xv[seq(s)]
        for i in range(3):
            product = dot(x_rows, r.wa[i])
            if i == 0:
                product = (product + r.hb[0:1]).astype(BF) * jnp.asarray(0.125, BF)
            elif i == 2:
                product = product + r.hb[1:2]
            r.qkv[i, seq(s)] = product.astype(BF)

    key_parts = [pl.ds(k * 128, 128) for k in range(SEQ // 128)]

    def attend(s, between=None):
        length = r.lengths[s]
        r.turned[...] = r.qkv[2, seq(s)].T

        def one_half(t, carry):
            q_rows = rows_of(s * SEQ + t * HALF, HALF)
            queries = r.qkv[0, q_rows]
            outs = []
            keys = r.qkv[1, seq(s)]
            visible = lax.broadcasted_iota(jnp.int32, (SEQ, HALF), 0) < length
            for h in range(3):
                scores = r.pulls.at[h % 2]
                found = dot_last(keys, queries * head_mask(h, BF))
                scores[...] = jnp.where(visible, found, -1000000000.0)
                top = jnp.max(scores[key_parts[0]], axis=0, keepdims=True)
                for part in key_parts[1:]:
                    top = jnp.maximum(top, jnp.max(scores[part], axis=0, keepdims=True))
                total = jnp.zeros((1, HALF), F32)
                for part in key_parts:
                    exponent = jnp.exp(scores[part] - top)
                    scores[part] = exponent
                    total += col_sum(exponent)
                inverse = 1.0 / total
                unit = 2 * (3 * s + h) + t
                for part in key_parts:
                    r.probs[unit, part] = (scores[part] * inverse).astype(BF)
                outs.append(dot(r.turned[HD * h : HD * (h + 1)], r.probs[unit]))
            total = pad_lanes(jnp.concatenate(outs, axis=0).T.astype(BF))
            r.mixed[q_rows] = total

            @pl.when(t == at.c)
            def _():
                r.o_all[at.m, s] = total

            if between is not None:
                pl.when(t == 0)(between)
            return carry

        lax.fori_loop(0, 2, one_half, 0)
        for i in range(3):
            o_copy(i, s).start()

    TILE = 32

    def for_tiles(body):
        def step(i, carry):
            body(pl.multiple_of(i * TILE, TILE))
            return carry

        lax.fori_loop(0, SEQ // TILE, step, 0, unroll=2)

    def eights(v):
        return jnp.sum(v.reshape(-1, 8, v.shape[1]), axis=0)

    def project_out(s):
        for i in range(3):
            o_copy(i, s).wait_recv()
        summed = r.xv[my_rows(s)].astype(F32) + r.vec[0:1]
        for m in range(4):
            summed += dot_last(r.o_all[m, s], r.wo_all[m])
        unit, inverse = norm_parts(summed)
        r.normal[mine(s)] = unit
        r.scale[mine(s)] = jnp.broadcast_to(inverse, (HALF, 128))
        r.low[my_rows(s)] = (unit * r.vec[1:2] + r.vec[2:3]).astype(BF)
        low_copy(s).start()

    def hidden(s):
        low_copy(s).wait_recv()
        r.dr[0:SEQ] = dot(r.low[seq(s)], r.wf[0].reshape(D, D))

        def tile(i):
            rows = rows_of(s * SEQ + i, TILE)
            for k in range(3):
                cols = pl.ds(256 * k, 256)
                up = r.dr[rows_of(i, TILE), cols] + r.ub[256 * k : 256 * (k + 1)].reshape(1, 256)
                bell = jnp.exp(up * up * -0.5)
                t = 1.0 / (1.0 + jnp.abs(up) * (0.3275911 * math.sqrt(0.5)))
                tail = 0.5 * 1.061405429 * t - 0.5 * 1.453152027
                for factor in (1.421413741, -0.284496736, 0.254829592):
                    tail = tail * t + 0.5 * factor
                tail = tail * t * bell
                phi = jnp.where(up < 0.0, tail, 1.0 - tail)
                r.z[rows, cols] = (up * phi).astype(BF)
                r.gp[rows, cols] = phi + up * (bell * (1.0 / math.sqrt(2.0 * math.pi)))

        for_tiles(tile)

    def sibling_rows(s):
        return rows_of(s * SEQ + (1 - at.c) * HALF, HALF)

    def both_halves(ref, s):
        return jnp.concatenate([ref[sibling_rows(s)], ref[my_rows(s)]], axis=0)

    def part_of(e, s, part):
        send_part(e, s, part[0:HALF])
        r.own[s % 2] = part[HALF:SEQ]

    def down(s):
        part_of(0, s, dot_last(both_halves(r.z, s), r.wf[1].reshape(D, D)))

    def out_far(s):
        return push(r.cv.at[s], r.out.at[my_rows(s)], r.outs.at[s], r.outr.at[s], at.sibling)

    def out_near(s):
        return pltpu.make_async_copy(r.cv.at[s], r.out.at[my_rows(s)], r.outl.at[s])

    def turn(s):
        c_load(s).wait()
        branch = whole(0, s)
        summed = r.normal[mine(s)] * r.vec[1:2] + r.vec[2:3] + branch + r.vec[3:4]
        unit, inverse = norm_parts(summed)
        cot = r.cv[s].astype(F32)
        grad = norm_back(cot, r.vec[4:5], unit, inverse)
        low_grad = grad.astype(BF)
        r.df[my_rows(s)] = low_grad
        df_copy(s).start()
        r.cv[s] = (unit * r.vec[4:5] + r.vec[5:6]).astype(BF)
        out_far(s).start()
        out_near(s).start()
        r.dr[mine(s)] = grad
        r.vec8[3] += eights(low_grad.astype(F32))
        r.vec8[4] += eights(cot * unit)
        r.vec8[5] += eights(cot)

    def feed_back(s):
        df_copy(s).wait_recv()
        pulled = dot(both_halves(r.df, s), r.wf[1].reshape(D, D)) * both_halves(r.gp, s)
        pulled = pulled.astype(BF)
        r.du[rows_of((1 - at.c) * HALF, HALF)] = pulled[0:HALF]
        r.du[rows_of(at.c * HALF, HALF)] = pulled[HALF:SEQ]
        part_of(1, s, dot_last(pulled, r.wf[0].reshape(D, D)))
        r.up8[...] += eights(pulled.astype(F32))

    def add_to(ref, index, value, first):
        if first:
            ref[index] = value
        else:
            ref[index] += value

    def feed_weights(s, w):
        left, right = (r.df, r.z[seq(s)]) if w else (r.low, r.du[...])
        for i in range(2):
            cols = pl.ds(i * 384, 384)
            term = dot_first(left[seq(s), cols], right).reshape(4, 96, D)
            add_to(r.dwf, (w, pl.ds(4 * i, 4)), term, s == 0)

    def fxs(w, i):
        return r.z.at[pl.ds((4 * w + i) * 96, 96)]

    def fzs(w, i):
        return r.low.at[pl.ds((3 * w + i - 1) * 96, 96)]

    def axs(i):
        return r.df.at[pl.ds(96 * i, 96)]

    def azs(i):
        return r.z.at[pl.ds(D + 96 * i, 96)]

    def beside_each_other(blocks):
        return jnp.concatenate(blocks, axis=1)

    def fx_copy(w, i):
        return push(fxs(w, i), r.fxr.at[w, i], r.fxss.at[w, i], r.fxrs.at[w, i], at.beside)

    def fz_copy(w, i):
        return push(
            fzs(w, i), r.fzr.at[w, i - 1], r.fzss.at[w, i - 1], r.fzrs.at[w, i - 1], at.along(i)
        )

    def ax_copy(i):
        return push(axs(i), r.axr.at[i], r.axss.at[i], r.axrs.at[i], at.beside)

    def az_copy(i):
        return push(azs(i), r.azr.at[i - 1], r.azss.at[i - 1], r.azrs.at[i - 1], at.along(i))

    sums_order = (1, 3, 2, 0)

    def feed_pairs_send(w):
        for i in sums_order:
            fxs(w, i)[...] = r.dwf[w, at.ahead(i, 1 - at.x)].astype(BF)
            fx_copy(w, i).start()

    def feed_pairs(w):
        for i in sums_order:
            fx_copy(w, i).wait_recv()
            pair = r.dwf[w, at.ahead(i, at.x)] + r.fxr[w, i].astype(F32)
            if i == 0:
                r.fsum[w] = pair
            else:
                fzs(w, i)[...] = pair.astype(BF)
                fz_copy(w, i).start()

    def feed_total(w):
        total = r.fsum[w]
        for i in (1, 2, 3):
            fz_copy(w, i).wait_recv()
            total += r.fzr[w, i - 1].astype(F32)
        r.fsum[w] = total

    def back(s):
        grad = r.dr[mine(s)] + whole(1, s)
        unit = r.normal[mine(s)]
        first = norm_back(grad, r.vec[1:2], unit, r.scale[mine(s)][:, 0:1])
        low_first = first.astype(BF)
        r.da[my_rows(s)] = low_first
        da_copy(s).start()
        r.dr[mine(s)] = first
        r.vec8[0] += eights(low_first.astype(F32))
        r.vec8[1] += eights(grad * unit)
        r.vec8[2] += eights(grad)

    def attend_back(s):
        r.turned[...] = r.qkv[1, seq(s)].T
        da_copy(s).wait_recv()
        r.do[...] = dot(r.da[seq(s)], r.wo_all[at.m, :, 0:wide]).astype(BF)

        def one_half(t, carry):
            here = rows_of(t * HALF, HALF)
            queries = r.qkv[0, rows_of(s * SEQ + t * HALF, HALF)]
            values = r.qkv[2, seq(s)]
            grad = r.do[here]
            outs, chances, grads_h, queries_h = [], [], [], []
            for h in range(3):
                mask = head_mask(h, BF)
                unit = 2 * (3 * s + h) + t
                grad_h = grad * mask
                pulls = r.pulls.at[h % 2]
                pulls[...] = dot_last(values, grad_h)
                inner = jnp.zeros((1, HALF), F32)
                for part in key_parts:
                    inner += col_sum(r.probs[unit, part].astype(F32) * pulls[part])
                cols = pl.ds(HALF * h, HALF)
                for part in key_parts:
                    slope = r.probs[unit, part].astype(F32) * (pulls[part] - inner)
                    r.du[part, cols] = slope.astype(BF)
                outs.append(dot(r.turned[HD * h : HD * (h + 1)], r.du[:, cols]))
                grads_h.append(grad_h)
                queries_h.append(queries * mask)
                chances.append(r.probs[unit])
            dq = jnp.concatenate(outs, axis=0).T
            r.dqkv[here, 0:wide] = (dq * 0.125).astype(BF)
            dk = dot(r.du[...], jnp.concatenate(queries_h, axis=0))
            dv = dot(jnp.concatenate(chances, axis=1), jnp.concatenate(grads_h, axis=0))

            @pl.when(t == 0)
            def _():
                r.dk[...] = dk
                r.dv[...] = dv

            @pl.when(t == 1)
            def _():
                r.dqkv[:, 256 : 256 + wide] = (r.dk[...] + dk).astype(BF)
                r.dqkv[:, 512 : 512 + wide] = (r.dv[...] + dv).astype(BF)

            return carry

        lax.fori_loop(0, 2, one_half, 0)

        halves = [
            jnp.concatenate(
                [
                    r.dqkv[rows_of((1 - at.c) * HALF, HALF), 256 * w : 256 * w + wide],
                    r.dqkv[rows_of(at.c * HALF, HALF), 256 * w : 256 * w + wide],
                ],
                axis=0,
            )
            for w in range(3)
        ]
        part = dot_last(halves[0], r.wa[0])
        part += dot_last(halves[1], r.wa[1])
        part += dot_last(halves[2], r.wa[2])
        part_of(2, s, part)
        r.head8[...] += eights(r.dqkv[...].astype(F32))

    def attend_weights(s):
        for i in range(3):
            cols = pl.ds(i * 256, 256)
            add_to(r.gp, cols, dot_first(r.xv[seq(s), cols], r.dqkv[...]), s == 0)
            term = dot_first(r.da[seq(s), cols], r.mixed[seq(s), 0:wide])
            add_to(r.gp, (pl.ds(D + i * 256, 256), pl.ds(0, wide)), term, s == 0)

    def gi_far(s):
        return push(r.ysend.at[s], r.cv.at[s], r.gs.at[s], r.gr.at[s], at.sibling)

    def gi_near(s):
        return pltpu.make_async_copy(r.ysend.at[s], r.gi.at[my_rows(s)], r.gl.at[s])

    def gi_other(s):
        return pltpu.make_async_copy(r.cv.at[s], r.gi.at[sibling_rows(s)], r.go.at[s])

    def finish(s):
        total = r.dr[mine(s)] + whole(2, s)
        far_copy(2, s).wait_send()
        r.ysend[s] = total.astype(BF)
        gi_far(s).start()
        gi_near(s).start()

    def attend_block(j):
        blocks = [r.gp[shard(j), 256 * w : 256 * w + wide] for w in range(3)]
        return beside_each_other(blocks + [r.gp[shard(8 + j), 0:wide]])

    def attend_pairs_send():
        for i in sums_order:
            j = at.ahead(i, 1 - at.x)
            axs(i)[...] = attend_block(j).astype(BF)
            ax_copy(i).start()

    def attend_pairs():
        for i in sums_order:
            ax_copy(i).wait_recv()
            pair = attend_block(at.ahead(i, at.x)) + r.axr[i].astype(F32)
            if i == 0:
                r.pair[...] = pair
            else:
                azs(i)[...] = pair.astype(BF)
                az_copy(i).start()

    def attend_total():
        total = r.pair[...]
        for i in (1, 2, 3):
            az_copy(i).wait_recv()
            total += r.azr[i - 1].astype(F32)
        for w in range(4):
            r.asum[w] = total[:, wide * w : wide * (w + 1)]

    def spread_dp(ref, send, recv):
        return [
            push(ref.at[at.d], ref.at[at.d], send.at[k - 1], recv.at[k - 1], dp_peer(k))
            for k in range(1, 8)
        ]

    def spread_mp(ref, send, recv):
        return [
            push(ref.at[at.m], ref.at[at.m], send.at[k - 1], recv.at[k - 1], mp_peer(k))
            for k in range(1, 4)
        ]

    def start(copies):
        for one in copies:
            one.start()

    def wait(copies):
        for one in copies:
            one.wait()

    def total_of(ref):
        total = ref[0]
        for i in range(1, ref.shape[0]):
            total += ref[i]
        return total

    pair_copy = push(r.vecp, r.vbox, r.vss, r.vrs, at.sibling)
    vec_copies = spread_dp(r.vecbox, r.vds, r.vdr)

    def spread_vec():
        pair_copy.wait()
        ups = col_sum(r.up8[...])
        pair = r.vecp[...] + r.vbox[...]
        for i in range(6):
            for k in range(6):
                r.vecbox[at.d, 6 * i + k : 6 * i + k + 1] = pair[i : i + 1, 128 * k : 128 * (k + 1)]
        for k in range(6):
            r.vecbox[at.d, 36 + k : 37 + k] = ups[:, 128 * k : 128 * (k + 1)]
        r.vecbox[at.d, 42:48] = jnp.zeros((6, 128), F32)
        start(vec_copies)

    small["aw"].wait()
    r.da[shard(at.d)] = jnp.concatenate([r.aw[i].astype(BF) for i in range(4)], axis=1)
    begin(0)
    x_copy(0, at.z).start()
    begin(1)
    x_copy(1, at.z).start()
    small["fw"].wait()
    for i in range(2):
        r.wf[i, at.d] = r.fw[i].astype(BF)
    x_copy(2, at.z).start()
    for name in MAIN_SMALL[2:]:
        small[name].wait()
    r.vec8[...] = jnp.zeros_like(r.vec8)
    r.up8[...] = jnp.zeros_like(r.up8)
    r.head8[...] = jnp.zeros_like(r.head8)
    r.dqkv[...] = jnp.zeros_like(r.dqkv)
    r.vecp[...] = jnp.zeros_like(r.vecp)
    step(0, 0)
    step(0, 1)
    begin(2)
    step(0, 2)
    for s in range(n_seq):
        x_load(s).wait()
    x_copy(3, at.z).start()
    for h in range(3):
        step(1, h)
    arrived(0)
    begin(3)
    for w in range(3):
        r.wa[w] = r.da[0:D, wide * w : wide * (w + 1)]
    project_in(0)
    spread_wo()
    step(2, 0)
    attend(0, lambda: step(2, 1))
    step(2, 2)
    project_in(1)
    hand_on_wo()
    step(3, 0)
    attend(1, lambda: step(3, 1))
    step(3, 2)
    for i in (0, 2):
        wo_copy(i).wait_recv()
    project_out(0)
    project_in(2)
    arrived(2)
    hidden(0)
    attend(2)
    project_out(1)
    arrived(3)
    down(0)
    hidden(1)
    pass_on(0, 0)
    down(1)
    project_out(2)
    pass_on(0, 1)
    hidden(2)
    down(2)
    for s in range(3, n_seq):
        project_in(s)
        attend(s)
        project_out(s)
        pass_on(0, s - 1)
        hidden(s)
        down(s)
    for g in range(4):
        sent(g)
    turn(0)
    pass_on(0, n_seq - 1)
    for s in range(n_seq):
        feed_back(s)
        if s < n_seq - 1:
            turn(s + 1)
            pass_on(1, s)
            feed_weights(s, 1)
            feed_weights(s, 0)
    for s in range(n_seq):
        low_copy(s).wait_send()
        df_copy(s).wait_send()
    feed_weights(n_seq - 1, 1)
    feed_pairs_send(1)
    pass_on(1, n_seq - 1)
    feed_weights(n_seq - 1, 0)
    feed_pairs_send(0)
    for s in range(n_seq):
        out_far(s).wait_send()
        out_near(s).wait()
    back(0)
    for s in range(n_seq):
        attend_back(s)
        if s == n_seq - 2:
            feed_pairs(1)
        if s < n_seq - 1:
            back(s + 1)
            pass_on(2, s)
            attend_weights(s)
        if s == n_seq - 2:
            feed_pairs(0)
    attend_weights(n_seq - 1)
    attend_pairs_send()
    pass_on(2, n_seq - 1)
    for i in range(6):
        r.vecp[i : i + 1] = col_sum(r.vec8[i])
    pair_copy.start()
    spread_vec()
    for s in range(n_seq - 1):
        finish(s)
    feed_total(1)
    feed_total(0)
    attend_pairs()
    grads = [r.asum.at[i] for i in range(4)] + [r.fsum.at[i] for i in range(2)]
    masters = [r.aw.at[i] for i in range(4)] + [r.fw.at[i] for i in range(2)]
    weight_squares = [sum_all(w[...] * w[...]) for w in masters]
    lanes = lax.broadcasted_iota(jnp.int32, (96, 128), 1)
    r.colbox[at.d] = jnp.zeros((COL_ROWS, 128), F32)

    def square_sums(i):
        square = grads[i][...] * grads[i][...] + 1e-30
        col = col_sum(square)
        if i < 4:
            r.colbox[at.d, 12 + 2 * i : 13 + 2 * i] = col[:, 0:128]
            r.colbox[at.d, 13 + 2 * i : 14 + 2 * i, 0:64] = col[:, 128:192]
        else:
            for k in range(6):
                place = 6 * (i - 4) + k
                r.colbox[at.d, place : place + 1] = col[:, 128 * k : 128 * (k + 1)]
        return jnp.where(lanes == i, jnp.sum(square, axis=1, keepdims=True), 0.0)

    columns = square_sums(4) + square_sums(5)
    attend_total()
    for i in range(4):
        columns += square_sums(i)
    heads = col_sum(r.head8[...])
    for i in range(2):
        r.colbox[at.d, 20 + 2 * i : 21 + 2 * i] = heads[:, 512 * i : 512 * i + 128]
        r.colbox[at.d, 21 + 2 * i : 22 + 2 * i, 0:64] = heads[:, 512 * i + 128 : 512 * i + 192]
    col_copies = spread_dp(r.colbox, r.cds, r.cdr)
    start(col_copies)
    r.flip[...] = jnp.zeros_like(r.flip)
    r.flip[0:96] = columns
    r.rowbox[at.m] = r.flip[...].T[0:8]
    row_copies = spread_mp(r.rowbox, r.rms, r.rmr)
    start(row_copies)
    finish(n_seq - 1)
    wait(vec_copies)
    vecs = total_of(r.vecbox)
    wait(row_copies)
    rows = total_of(r.rowbox)
    wait(col_copies)
    cols = total_of(r.colbox)
    arow, frow, col_news = new_moments(r, cols, rows)
    r.flip[...] = jnp.zeros_like(r.flip)
    r.flip[0:4, 0:96] = arow
    r.flip[4:6, 0:96] = frow
    turned = r.flip[...].T
    row_news = [turned[0:96, i : i + 1] for i in range(6)]
    head, head_state, head_step, up, up_state, up_step = bias_steps(r, cols, vecs)
    tile_rows = lax.broadcasted_iota(jnp.int32, (8, 128), 0)
    tile_lanes = lax.broadcasted_iota(jnp.int32, (8, 128), 1)
    tile = jnp.zeros((8, 128), F32)

    def put(tile, row, lane, value):
        return jnp.where((tile_rows == row) & (tile_lanes == lane), value, tile)

    for i in range(6):
        square = grads[i][...] * grads[i][...]
        tile = put(tile, 0, i, sum_all(row_news[i]))
        tile = put(tile, 1, i, sum_all(square / (row_news[i] * col_news[i])))
        tile = put(tile, 2, i, weight_squares[i])
    for i in range(2):
        tile = put(tile, 3, i, sum_all(head_step[i : i + 1] * head_step[i : i + 1]))
        tile = put(tile, 4, i, sum_all(r.hb[i : i + 1] * r.hb[i : i + 1]))
    ub = r.ub[...].reshape(1, D)
    tile = put(tile, 3, 2, sum_all(up_step * up_step))
    tile = put(tile, 4, 2, sum_all(ub * ub))
    r.statm[at.m] = tile
    mp_copies = spread_mp(r.statm, r.sms, r.smr)
    start(mp_copies)
    r.sums[0:VEC_ROWS] = vecs
    r.sums[VEC_ROWS : VEC_ROWS + COL_ROWS] = cols
    r.sums[72:80] = rows
    wait(mp_copies)
    group = total_of(r.statm)
    r.statd[at.d] = group
    dp_copies = spread_dp(r.statd, r.sds, r.sdr)
    start(dp_copies)
    r.sums[80:88] = group
    for s in range(n_seq):
        out_far(s).wait_recv()
        gi_far(s).wait()
        gi_other(s).start()
        gi_near(s).wait()
        core_copy(2, s).wait_send()
        da_copy(s).wait_send()
        for i in range(3):
            o_copy(i, s).wait_send()
    for i in range(3):
        wo_copy(i).wait_send()
    for i in range(4):
        ax_copy(i).wait_send()
        for w in range(2):
            fx_copy(w, i).wait_send()
            if i > 0:
                fz_copy(w, i).wait_send()
        if i > 0:
            az_copy(i).wait_send()
    for s in range(n_seq):
        gi_other(s).wait()
    wait(dp_copies)
    r.sums[88:96] = total_of(r.statd)


LAST_SMALL = (
    "asum", "fsum", "sums", "aw", "fw", "vec", "hb", "ars", "acs", "frs", "fcs", "vst", "hst",
)
LAST_IN = ("out_from", "gi_from", "ub", "ust") + tuple("far_" + name for name in LAST_SMALL)
LAST_NEW = (
    "agrad", "anew", "arow", "acol", "fgrad", "fnew", "frow", "fcol", "vgrad", "vsnew", "vnew",
    "hgrad", "hsnew", "hnew",
)
LAST_OUT = ("out", "gi") + tuple("to_" + name for name in LAST_NEW) + ("ugrad", "usnew", "unew")


def moved(weight, update, mean_update, mean_weight):
    clip = jnp.maximum(1.0, jnp.sqrt(mean_update) * (1.0 / clip_limit))
    size = jnp.maximum(0.001, jnp.sqrt(mean_weight))
    return weight - update * (rate * size / clip)


def last_kernel(names, *refs):
    r = Refs(names, refs)
    pieces = r.copied.shape[1]
    size = r.out_from.shape[0] // pieces
    parts = [pl.ds(i * size, size) for i in range(pieces)]
    small = fetched(LAST_SMALL, r, r.small)
    for one in small.values():
        one.start()
    gi_in, gi_out, out_in, out_out = [
        [
            pltpu.make_async_copy(src.at[part], dst.at[part], r.copied.at[k, i])
            for i, part in enumerate(parts)
        ]
        for k, (src, dst) in enumerate(
            (
                (r.gi_from, r.gi_low),
                (r.gi_via, r.gi),
                (r.out_from, r.out_via),
                (r.out_via, r.out),
            )
        )
    ]
    for one in gi_in + out_in:
        one.start()
    for i, part in enumerate(parts):
        gi_in[i].wait()
        r.gi_via[part] = r.gi_low[part].astype(F32)
        gi_out[i].start()
    for i in range(pieces):
        out_in[i].wait()
        out_out[i].start()
    for one in small.values():
        one.wait()
    vecs = r.sums[0:VEC_ROWS]
    cols = r.sums[VEC_ROWS : VEC_ROWS + COL_ROWS]
    rows = r.sums[72:80]
    group = r.sums[80:88]
    everything = r.sums[88:96]
    arow, frow, col_news = new_moments(r, cols, rows)
    r.arow[...] = arow
    r.frow[...] = frow
    for i in range(4):
        r.acol[i : i + 1] = col_news[i]
    for i in range(2):
        r.fcol[i : i + 1] = col_news[4 + i]
    r.flip[...] = jnp.zeros_like(r.flip)
    r.flip[0:4, 0:96] = arow
    r.flip[4:6, 0:96] = frow
    turned = r.flip[...].T
    head, head_state, head_step, up, up_state, up_step = bias_steps(r, cols, vecs)
    r.hgrad[...] = head
    r.hsnew[...] = head_state
    r.ugrad[...] = up.reshape(D)
    r.usnew[...] = up_state.reshape(D)
    ub = r.ub[...].reshape(1, D)
    for i in range(2):
        r.hnew[i : i + 1] = moved(
            r.hb[i : i + 1],
            head_step[i : i + 1],
            group[3:4, i : i + 1] * (1.0 / D),
            group[4:5, i : i + 1] * (1.0 / D),
        )
    unew = moved(ub, up_step, group[3:4, 2:3] * (1.0 / FF), group[4:5, 2:3] * (1.0 / FF))
    r.unew[...] = unew.reshape(D)
    for i in range(6):
        r.vgrad[i : i + 1] = jnp.concatenate(
            [vecs[6 * i + k : 6 * i + k + 1] for k in range(6)], axis=1
        )
    decay, keep = adafactor_rates()
    vec_grad = r.vgrad[...]
    vec_state = decay * r.vst[...] + keep * (vec_grad * vec_grad + 1e-30)
    r.vsnew[...] = vec_state
    vec_step = vec_grad * lax.rsqrt(vec_state)
    r.vnew[...] = moved(
        r.vec[...],
        vec_step,
        jnp.sum(vec_step * vec_step, axis=1, keepdims=True) * (1.0 / D),
        jnp.sum(r.vec[...] * r.vec[...], axis=1, keepdims=True) * (1.0 / D),
    )
    r.agrad[...] = r.asum[...]
    r.fgrad[...] = r.fsum[...]
    for i in range(6):
        count = float(D * (D if i < 4 else FF))
        grad, master, new = (
            (r.asum.at[i], r.aw.at[i], r.anew.at[i])
            if i < 4
            else (r.fsum.at[i - 4], r.fw.at[i - 4], r.fnew.at[i - 4])
        )
        average = everything[0:1, i : i + 1] * (1.0 / (4 * D))
        product = turned[0:96, i : i + 1] * col_news[i]
        step = grad[...] * lax.rsqrt(product / average)
        new[...] = moved(
            master[...],
            step,
            average * everything[1:2, i : i + 1] * (1.0 / count),
            everything[2:3, i : i + 1] * (1.0 / count),
        )
    given = {
        name: pltpu.make_async_copy(r.__dict__[name], r.__dict__["to_" + name], r.given.at[i])
        for i, name in enumerate(LAST_NEW)
    }
    for one in given.values():
        one.start()
    for one in list(given.values()) + gi_out + out_out:
        one.wait()


def dma(*shape):
    return pltpu.SemaphoreType.DMA(shape) if shape else pltpu.SemaphoreType.DMA


def specs_of(names, spaces, rest):
    return [pl.BlockSpec(memory_space=spaces.get(name, rest)) for name in names]


def on_device_kernels(
    tokens, cotangent, lengths, attn_weights, ffn_weights, row_vectors, head_bias, up_bias,
    attn_row_state, attn_col_state, ffn_row_state, ffn_col_state, vec_state, head_bias_state,
    up_bias_state,
):
    rows = tokens.shape[0]
    n_seq = lengths.shape[0]
    wide = 3 * HD
    scratch = main_scratch(n_seq)
    out, grad_input, attn_sum, ffn_sum, sums = pl.pallas_call(
        functools.partial(main_kernel, n_seq, MAIN_IN + MAIN_OUT + tuple(scratch)),
        out_shape=[
            jax.ShapeDtypeStruct((rows, D), BF),
            jax.ShapeDtypeStruct((rows, D), BF),
            jax.ShapeDtypeStruct((4, 96, wide), F32),
            jax.ShapeDtypeStruct((2, 96, D), F32),
            jax.ShapeDtypeStruct((96, 128), F32),
        ],
        in_specs=specs_of(MAIN_IN, dict(lengths=pltpu.SMEM, ub=pltpu.VMEM, ust=pltpu.VMEM), pl.ANY),
        out_specs=specs_of(MAIN_OUT, dict(out=pl.ANY, gi=pl.ANY), pltpu.VMEM),
        scratch_shapes=list(scratch.values()),
        compiler_params=pltpu.CompilerParams(
            collective_id=0, has_side_effects=True, vmem_limit_bytes=VMEM_BYTES
        ),
    )(
        tokens, cotangent, lengths, up_bias, up_bias_state, attn_weights, ffn_weights, row_vectors,
        head_bias, attn_row_state, attn_col_state, ffn_row_state, ffn_col_state, head_bias_state,
    )
    results = {
        "out": ((rows, D), BF),
        "gi": ((rows, D), F32),
        "agrad": ((4, 96, wide), F32),
        "anew": ((4, 96, wide), F32),
        "arow": ((4, 96), F32),
        "acol": ((4, wide), F32),
        "fgrad": ((2, 96, D), F32),
        "fnew": ((2, 96, D), F32),
        "frow": ((2, 96), F32),
        "fcol": ((2, D), F32),
        "vgrad": ((6, D), F32),
        "vsnew": ((6, D), F32),
        "vnew": ((6, D), F32),
        "hgrad": ((2, wide), F32),
        "hsnew": ((2, wide), F32),
        "hnew": ((2, wide), F32),
        "ugrad": ((D,), F32),
        "usnew": ((D,), F32),
        "unew": ((D,), F32),
    }
    shapes = dict(
        asum=(4, 96, wide), fsum=(2, 96, D), sums=(96, 128), aw=(4, 96, wide), fw=(2, 96, D),
        vec=(6, D), hb=(2, wide), ars=(4, 96), acs=(4, wide), frs=(2, 96), fcs=(2, D), vst=(6, D),
        hst=(2, wide),
    )
    boxes = {name: pltpu.VMEM(shapes[name], F32) for name in LAST_SMALL}
    boxes.update({name: pltpu.VMEM(results[name][0], F32) for name in LAST_NEW})
    boxes.update(
        flip=pltpu.VMEM((128, 128), F32),
        out_via=pltpu.VMEM((rows, D), BF),
        gi_low=pltpu.VMEM((rows, D), BF),
        gi_via=pltpu.VMEM((rows, D), F32),
        copied=dma(4, 4),
        small=dma(len(LAST_SMALL)),
        given=dma(len(LAST_NEW)),
    )
    straight = dict(ub=pltpu.VMEM, ust=pltpu.VMEM, ugrad=pltpu.VMEM, usnew=pltpu.VMEM, unew=pltpu.VMEM)
    return tuple(
        pl.pallas_call(
            functools.partial(last_kernel, LAST_IN + LAST_OUT + tuple(boxes)),
            out_shape=[
                jax.ShapeDtypeStruct(*results[name.removeprefix("to_")]) for name in LAST_OUT
            ],
            in_specs=specs_of(LAST_IN, straight, pl.ANY),
            out_specs=specs_of(LAST_OUT, straight, pl.ANY),
            scratch_shapes=list(boxes.values()),
            compiler_params=pltpu.CompilerParams(vmem_limit_bytes=VMEM_BYTES),
        )(
            out, grad_input, up_bias, up_bias_state, attn_sum, ffn_sum, sums, attn_weights,
            ffn_weights, row_vectors, head_bias, attn_row_state, attn_col_state, ffn_row_state,
            ffn_col_state, vec_state, head_bias_state,
        )
    )


def layer_norm(summed, norm_gain, norm_shift):
    average = jnp.mean(summed, axis=-1, keepdims=True)
    centered = summed - average
    variance = jnp.mean(centered * centered, axis=-1, keepdims=True)
    return centered * lax.rsqrt(variance + 1e-12) * norm_gain + norm_shift


def gelu_exact(argument):
    return jax.nn.gelu(argument, approximate=False)


def project(left, right):
    return jnp.dot(left, right, preferred_element_type=jnp.float32)


def contract_rows(left, right):
    return lax.dot_general(
        left, right, (((0,), (0,)), ((), ())), preferred_element_type=jnp.float32
    )


def contract_last(left, right):
    return lax.dot_general(
        left, right, (((1,), (1,)), ((), ())), preferred_element_type=jnp.float32
    )


def scores_for(queries, key_rows, length):
    score_scale = 1.0 / math.sqrt(HD)
    scores = (
        jnp.einsum("qhd,khd->hqk", queries, key_rows, preferred_element_type=jnp.float32)
        * score_scale
    )
    visible = lax.broadcasted_iota(jnp.int32, (1, 1, SEQ), 2) < length
    return jnp.where(visible, scores, -1000000000.0)


def attend_forward(element):
    queries, key_rows, values, length = element
    scores = scores_for(queries, key_rows, length)
    row_max = jnp.max(scores, axis=2, keepdims=True)
    exponent = jnp.exp(scores - row_max)
    denominator = jnp.sum(exponent, axis=2, keepdims=True)
    attn_probs = (exponent / denominator).astype(jnp.bfloat16)
    mixed = jnp.einsum("hqk,khd->qhd", attn_probs, values, preferred_element_type=jnp.float32)
    return (mixed.astype(jnp.bfloat16), row_max + jnp.log(denominator))


def attend_backward(element):
    queries, key_rows, values, length, log_total, grad_mixed = element
    score_scale = 1.0 / math.sqrt(HD)
    attn_probs = jnp.exp(scores_for(queries, key_rows, length) - log_total)
    grad_probs = jnp.einsum("qhd,khd->hqk", grad_mixed, values, preferred_element_type=jnp.float32)
    inner = jnp.sum(attn_probs * grad_probs, axis=2, keepdims=True)
    grad_scores = (attn_probs * (grad_probs - inner)).astype(jnp.bfloat16)
    grad_queries = (
        jnp.einsum("hqk,khd->qhd", grad_scores, key_rows, preferred_element_type=jnp.float32)
        * score_scale
    )
    grad_keys = (
        jnp.einsum("hqk,qhd->khd", grad_scores, queries, preferred_element_type=jnp.float32)
        * score_scale
    )
    grad_values = jnp.einsum(
        "hqk,qhd->khd",
        attn_probs.astype(jnp.bfloat16),
        grad_mixed,
        preferred_element_type=jnp.float32,
    )
    return (
        grad_queries.astype(jnp.bfloat16),
        grad_keys.astype(jnp.bfloat16),
        grad_values.astype(jnp.bfloat16),
    )


def attention_block(tokens, attn_full, head_bias, lengths):
    local_cols = attn_full.shape[2]
    split_shape = (lengths.shape[0], SEQ, local_cols // HD, HD)
    bias_rows = jnp.stack([head_bias[0], jnp.zeros_like(head_bias[0]), head_bias[1]])
    stacked = jnp.einsum("rd,sdc->src", tokens, attn_full[:3], preferred_element_type=jnp.float32)
    qkv_low = (stacked + bias_rows[:, None, :]).astype(jnp.bfloat16)
    mixed, log_total = lax.map(
        attend_forward,
        (
            qkv_low[0].reshape(split_shape),
            qkv_low[1].reshape(split_shape),
            qkv_low[2].reshape(split_shape),
            lengths,
        ),
    )
    return (qkv_low, mixed.reshape(tokens.shape[0], local_cols), log_total)


def up_block(normed_low, ffn_full, up_bias):
    hidden = project(normed_low, ffn_full[0]) + up_bias
    activated, gelu_pull = jax.vjp(gelu_exact, hidden)
    return (activated.astype(jnp.bfloat16), gelu_pull)


def apply_clip(weight, update, mean_update, mean_weight):
    clip_factor = jnp.maximum(1.0, jnp.sqrt(mean_update) / clip_limit)
    step_size = jnp.maximum(0.001, jnp.sqrt(mean_weight))
    return weight - rate * step_size * update / clip_factor


def on_device(
    tokens,
    cotangent,
    lengths,
    attn_weights,
    ffn_weights,
    row_vectors,
    head_bias,
    up_bias,
    attn_row_state,
    attn_col_state,
    ffn_row_state,
    ffn_col_state,
    vec_state,
    head_bias_state,
    up_bias_state,
):
    attn_full, ffn_full = (
        lax.all_gather(attn_weights.astype(jnp.bfloat16), "dp", axis=1, tiled=True),
        lax.all_gather(ffn_weights.astype(jnp.bfloat16), "dp", axis=1, tiled=True),
    )
    row_count = tokens.shape[0]
    local_cols = attn_full.shape[2]
    split_shape = (lengths.shape[0], SEQ, local_cols // HD, HD)
    qkv_low, mixed_low, log_total = attention_block(tokens, attn_full, head_bias, lengths)
    attn_terms = contract_last(mixed_low, attn_full[3])
    attended = lax.psum(attn_terms, "mp") + row_vectors[0]
    residual_in = tokens.astype(jnp.float32)
    normed, first_pull = jax.vjp(layer_norm, residual_in + attended, row_vectors[1], row_vectors[2])
    normed_low = normed.astype(jnp.bfloat16)
    act_low, gelu_pull = up_block(normed_low, ffn_full, up_bias)
    ffn_terms = contract_last(act_low, ffn_full[1])
    branch = lax.psum(ffn_terms, "mp") + row_vectors[3]
    result, second_pull = jax.vjp(layer_norm, normed + branch, row_vectors[4], row_vectors[5])
    result_low = result.astype(jnp.bfloat16)
    grad_second, gain_second, shift_second = second_pull(cotangent.astype(jnp.float32))
    act_back, gelu_back = up_block(normed_low, ffn_full, up_bias)
    grad_branch = grad_second.astype(jnp.bfloat16)
    down_grad = contract_rows(grad_branch, act_back)
    bias_down = jnp.sum(grad_branch, axis=0, dtype=jnp.float32)
    (grad_hidden,) = gelu_back(project(grad_branch, ffn_full[1]))
    grad_hidden = grad_hidden.astype(jnp.bfloat16)
    up_grad = contract_rows(normed_low, grad_hidden)
    bias_up = jnp.sum(grad_hidden, axis=0, dtype=jnp.float32)
    ffn_grads = jnp.stack([up_grad, down_grad])
    ffn_input = contract_last(grad_hidden, ffn_full[0])
    grad_normed = grad_second + lax.psum(ffn_input, "mp")
    grad_first, gain_first, shift_first = first_pull(grad_normed)
    qkv_back, mixed_back, total_back = attention_block(tokens, attn_full, head_bias, lengths)
    grad_attended = grad_first.astype(jnp.bfloat16)
    out_grad = contract_rows(grad_attended, mixed_back)
    bias_out = jnp.sum(grad_attended, axis=0, dtype=jnp.float32)
    grad_mixed = project(grad_attended, attn_full[3]).astype(jnp.bfloat16)
    grad_queries, grad_keys, grad_values = lax.map(
        attend_backward,
        (
            qkv_back[0].reshape(split_shape),
            qkv_back[1].reshape(split_shape),
            qkv_back[2].reshape(split_shape),
            lengths,
            total_back,
            grad_mixed.reshape(split_shape),
        ),
    )
    qkv_grads = jnp.stack(
        [
            grad_queries.reshape(row_count, local_cols),
            grad_keys.reshape(row_count, local_cols),
            grad_values.reshape(row_count, local_cols),
        ]
    )
    proj_grads = jnp.einsum("rd,src->sdc", tokens, qkv_grads, preferred_element_type=jnp.float32)
    attn_grads = jnp.concatenate([proj_grads, out_grad[None]], axis=0)
    attn_input = jnp.einsum(
        "src,sdc->rd", qkv_grads, attn_full[:3], preferred_element_type=jnp.float32
    )
    norm_part = jnp.stack([gain_first, shift_first, gain_second, shift_second])
    grad_input = grad_first + lax.psum(attn_input, "mp")
    head_grads = jnp.stack(
        [
            jnp.sum(qkv_grads[0], axis=0, dtype=jnp.float32),
            jnp.sum(qkv_grads[2], axis=0, dtype=jnp.float32),
        ]
    )
    vec_grads = jnp.stack(
        [bias_out, norm_part[0], norm_part[1], bias_down, norm_part[2], norm_part[3]]
    )
    attn_sum, ffn_sum = (
        lax.psum_scatter(attn_grads, "dp", scatter_dimension=1, tiled=True),
        lax.psum_scatter(ffn_grads, "dp", scatter_dimension=1, tiled=True),
    )
    decay_rate = 1.0 - STEP ** (-0.8)
    keep_rate = 1.0 - decay_rate
    attn_square = attn_sum * attn_sum + 1e-30
    ffn_square = ffn_sum * ffn_sum + 1e-30
    vec_sum, head_sum, up_sum, attn_cols, ffn_cols = lax.psum(
        (vec_grads, head_grads, bias_up, jnp.sum(attn_square, axis=1), jnp.sum(ffn_square, axis=1)),
        "dp",
    )
    attn_rows, ffn_rows = lax.psum(
        (jnp.sum(attn_square, axis=2), jnp.sum(ffn_square, axis=2)), "mp"
    )
    attn_row_new = decay_rate * attn_row_state + keep_rate * (attn_rows / D)
    attn_col_new = decay_rate * attn_col_state + keep_rate * (attn_cols / D)
    ffn_row_new = decay_rate * ffn_row_state + keep_rate * (ffn_rows / FF)
    ffn_col_new = decay_rate * ffn_col_state + keep_rate * (ffn_cols / D)
    vec_state_new = decay_rate * vec_state + keep_rate * (vec_sum * vec_sum + 1e-30)
    vec_step = vec_sum * lax.rsqrt(vec_state_new)
    vec_new = apply_clip(
        row_vectors,
        vec_step,
        jnp.mean(vec_step * vec_step, axis=1)[:, None],
        jnp.mean(row_vectors * row_vectors, axis=1)[:, None],
    )
    head_state_new = decay_rate * head_bias_state + keep_rate * (head_sum * head_sum + 1e-30)
    head_step = head_sum * lax.rsqrt(head_state_new)
    up_state_new = decay_rate * up_bias_state + keep_rate * (up_sum * up_sum + 1e-30)
    up_step = up_sum * lax.rsqrt(up_state_new)
    attn_ratio = jnp.sum(
        attn_sum * attn_sum / (attn_row_new[:, :, None] * attn_col_new[:, None, :]), axis=(1, 2)
    )
    ffn_ratio = jnp.sum(
        ffn_sum * ffn_sum / (ffn_row_new[:, :, None] * ffn_col_new[:, None, :]), axis=(1, 2)
    )
    attn_stats = jnp.stack(
        [
            jnp.sum(attn_row_new, axis=1),
            attn_ratio,
            jnp.sum(attn_weights * attn_weights, axis=(1, 2)),
        ]
    )
    ffn_stats = jnp.stack(
        [jnp.sum(ffn_row_new, axis=1), ffn_ratio, jnp.sum(ffn_weights * ffn_weights, axis=(1, 2))]
    )
    bias_stats = jnp.stack(
        [
            jnp.concatenate(
                [jnp.sum(head_step * head_step, axis=1), jnp.sum(up_step * up_step)[None]]
            ),
            jnp.concatenate(
                [jnp.sum(head_bias * head_bias, axis=1), jnp.sum(up_bias * up_bias)[None]]
            ),
        ]
    )
    attn_total, ffn_total, bias_total = lax.psum((attn_stats, ffn_stats, bias_stats), ("dp", "mp"))
    mp_count = lax.axis_size("mp")
    dp_count = lax.axis_size("dp")
    attn_average = attn_total[0] / (mp_count * D)
    attn_step = attn_sum * lax.rsqrt(
        attn_row_new[:, :, None] * attn_col_new[:, None, :] / attn_average[:, None, None]
    )
    attn_new = apply_clip(
        attn_weights,
        attn_step,
        (attn_average * attn_total[1] / (D * D))[:, None, None],
        (attn_total[2] / (D * D))[:, None, None],
    )
    ffn_average = ffn_total[0] / (mp_count * D)
    ffn_step = ffn_sum * lax.rsqrt(
        ffn_row_new[:, :, None] * ffn_col_new[:, None, :] / ffn_average[:, None, None]
    )
    ffn_new = apply_clip(
        ffn_weights,
        ffn_step,
        (ffn_average * ffn_total[1] / (D * FF))[:, None, None],
        (ffn_total[2] / (D * FF))[:, None, None],
    )
    counts = jnp.asarray([D, D, FF], jnp.float32) * dp_count
    update_means = bias_total[0] / counts
    weight_means = bias_total[1] / counts
    head_new = apply_clip(head_bias, head_step, update_means[:2, None], weight_means[:2, None])
    up_new = apply_clip(up_bias, up_step, update_means[2], weight_means[2])
    return (
        result_low,
        grad_input,
        attn_sum,
        attn_new,
        attn_row_new,
        attn_col_new,
        ffn_sum,
        ffn_new,
        ffn_row_new,
        ffn_col_new,
        vec_sum,
        vec_state_new,
        vec_new,
        head_sum,
        head_state_new,
        head_new,
        up_sum,
        up_state_new,
        up_new,
    )


def solution(mesh):
    in_specs = (
        P("dp", None),
        P("dp", None),
        P("dp"),
        P(None, "dp", "mp"),
        P(None, "dp", "mp"),
        P(),
        P(None, "mp"),
        P("mp"),
        P(None, "dp"),
        P(None, "mp"),
        P(None, "dp"),
        P(None, "mp"),
        P(),
        P(None, "mp"),
        P("mp"),
    )
    out_specs = (
        P("dp", None),
        P("dp", None),
        P(None, "dp", "mp"),
        P(None, "dp", "mp"),
        P(None, "dp"),
        P(None, "mp"),
        P(None, "dp", "mp"),
        P(None, "dp", "mp"),
        P(None, "dp"),
        P(None, "mp"),
        P(),
        P(),
        P(),
        P(None, "mp"),
        P(None, "mp"),
        P(None, "mp"),
        P("mp"),
        P("mp"),
        P("mp"),
    )
    def device_program(*arrays):
        fits = mesh.shape["dp"] == 8 and mesh.shape["mp"] == 4 and arrays[2].shape[0] == 3
        return (on_device_kernels if fits else on_device)(*arrays)

    return jax.shard_map(
        device_program, mesh=mesh, in_specs=in_specs, out_specs=out_specs, check_vma=False
    )
```
